32 devices in a mesh: groups: 2 (over y), cluster: 8 (over z, x), inner: 2 (over core).
Axes of the slice: x: 2, y: 2, z: 4, core: 2. Of those that a mesh axis runs over, the one named last changes fastest.
Arguments:
- right_sides: float32 [64, 65536], P(None, ('groups', 'cluster', 'inner')), parts along dimension 1, may hold values from -6 to 6
- tree_order: int32 [16, 2048], P(('cluster', 'inner')), may hold values from 0 to 2047, each once within a row
- leaf_inverse: float32 [128, 256, 256], P(('cluster', 'inner')), may hold values from -0.375 to 0.375
- reduce_low: float32 [128, 32768], P(None, ('cluster', 'inner')), may hold values from -0.09375 to 0.09375
- expand_low: float32 [128, 32768], P(None, ('cluster', 'inner')), may hold values from -0.5 to 0.5
- reduce_mid: float32 [128, 32768], P(None, ('cluster', 'inner')), may hold values from -0.0625 to 0.0625
- expand_mid: float32 [128, 32768], P(None, ('cluster', 'inner')), may hold values from -0.5 to 0.5
- reduce_top: float32 [128, 32768], P(None, ('cluster', 'inner')), may hold values from -0.046875 to 0.046875
- expand_top: float32 [128, 32768], P(None, ('cluster', 'inner')), may hold values from -0.5 to 0.5
- coupling_low: float32 [4, 256, 256], replicated, may hold values from -0.375 to 0.375
- coupling_mid: float32 [2, 256, 256], replicated, may hold values from -0.375 to 0.375
- coupling_top: float32 [1, 256, 256], replicated, may hold values from -0.375 to 0.375
Outputs:
- solution: float32 [64, 65536], P(None, ('groups', 'cluster', 'inner')), parts along dimension 1
The draws below stay inside these ranges and needn't reach their ends.
There are 2 independent parts, one for each index of `groups`. The reference program is written for one: setup_inputs(seed, part) draws one part's arguments, and reference() takes and returns one part's arrays. A program takes and returns all parts, laid end to end along the dimension named above; an argument that names none is the same for every part. Nothing has to cross between parts.
Inputs may be any that keep to these rules, and one draw needn't show every extreme that they name: Each row of tree_order is a permutation of 0 to 2047.
All inputs are finite; a program needn't handle non-finite values.
Results may differ from the reference program's by a relative error of at most 0.000082.
Values sent between devices are 32-bit elements; how exact they have to be, the bound alone decides.
A program may use at most 64 MiB of HBM per device.

```python
import jax
import jax.numpy as jnp
from jax import lax

M_DEV = 2048
RHS = 64
R = 128
LEAF = 256
DEVS = 16
ROWS = 32768
LEAFS = 128


def block_scale(key, extent, cuts, low, largest):
    def one(position, shards_of):
        steps = jax.random.uniform(jax.random.fold_in(jax.random.fold_in(key, 6), position), (shards_of,), jnp.float32, low / len(cuts), largest / len(cuts))
        return jnp.repeat(jnp.exp(steps), extent[position] // shards_of).reshape((-1,) + (1,) * (len(extent) - position - 1))

    level = one(*cuts[0])
    for cut in cuts[1:]:
        level = level * one(*cut)
    return level


def scatter_about(rng, dims, width, limit, cuts=(), held_as=jnp.bfloat16):
    entries = jax.random.normal(rng, dims, jnp.float32) * width
    if len(cuts) > 0:
        entries = block_scale(rng, dims, cuts, -0.22, 0.18) * entries
    return jnp.clip(entries, min=-limit, max=limit).astype(held_as)


def setup_inputs(seed: int = 0, part: int = 0) -> dict:
    key_of = jax.random.split(jax.random.key(seed), 13)
    part_splits = jax.random.split(jax.random.fold_in(key_of[12], part), 13)
    right_sides = scatter_about(part_splits[0], (RHS, ROWS), 1.0, 6.0, ((1, 16),), jnp.float32)
    tree_order = jax.vmap(lambda own: jax.random.permutation(own, M_DEV))(jax.random.split(key_of[1], DEVS)).reshape((DEVS, M_DEV)).astype(jnp.int32)
    leaf_inverse = scatter_about(key_of[2], (LEAFS, LEAF, LEAF), LEAF ** -0.5, 0.375, ((0, 16),), jnp.float32)
    reduce_low = scatter_about(key_of[3], (R, ROWS), (ROWS // 8) ** -0.5, 0.09375, ((1, 16),), jnp.float32)
    expand_low = scatter_about(key_of[4], (R, ROWS), R ** -0.5, 0.5, ((1, 16),), jnp.float32)
    reduce_mid = scatter_about(key_of[5], (R, ROWS), (ROWS // 4) ** -0.5, 0.0625, ((1, 16),), jnp.float32)
    expand_mid = scatter_about(key_of[6], (R, ROWS), R ** -0.5, 0.5, ((1, 16),), jnp.float32)
    reduce_top = scatter_about(key_of[7], (R, ROWS), (ROWS // 2) ** -0.5, 0.046875, ((1, 16),), jnp.float32)
    expand_top = scatter_about(key_of[8], (R, ROWS), R ** -0.5, 0.5, ((1, 16),), jnp.float32)
    coupling_low = scatter_about(key_of[9], (4, 2 * R, 2 * R), (2 * R) ** -0.5, 0.375, (), jnp.float32)
    coupling_mid = scatter_about(key_of[10], (2, 2 * R, 2 * R), (2 * R) ** -0.5, 0.375, (), jnp.float32)
    coupling_top = scatter_about(key_of[11], (1, 2 * R, 2 * R), (2 * R) ** -0.5, 0.375, (), jnp.float32)
    return dict(right_sides=right_sides, tree_order=tree_order, leaf_inverse=leaf_inverse, reduce_low=reduce_low, expand_low=expand_low, reduce_mid=reduce_mid, expand_mid=expand_mid, reduce_top=reduce_top, expand_top=expand_top, coupling_low=coupling_low, coupling_mid=coupling_mid, coupling_top=coupling_top)


HIGH = lax.Precision.HIGHEST


def apply_level(field, reduce_basis, expand_basis, coupling, level):
    children = 2 ** level
    nodes = children // 2
    rhs_count = field.shape[0]
    rank = reduce_basis.shape[0]
    blocks = field.reshape(rhs_count, children, -1)
    reduce_blocks = reduce_basis.reshape(rank, children, -1)
    expand_blocks = expand_basis.reshape(rank, children, -1)
    coeffs = jnp.einsum('rcm,kcm->crk', blocks, reduce_blocks, precision=HIGH)
    stacked = coeffs.reshape(nodes, 2, rhs_count, rank).transpose(0, 2, 1, 3).reshape(nodes, rhs_count, 2 * rank)
    solved = jnp.einsum('nrj,nij->nri', stacked, coupling, precision=HIGH)
    halves = solved.reshape(nodes, rhs_count, 2, rank).transpose(0, 2, 1, 3).reshape(children, rhs_count, rank)
    update = jnp.einsum('crk,kcm->rcm', halves, expand_blocks, precision=HIGH)
    return (blocks - update).reshape(rhs_count, -1)


def reference(right_sides, tree_order, leaf_inverse, reduce_low, expand_low, reduce_mid, expand_mid, reduce_top, expand_top, coupling_low, coupling_mid, coupling_top):
    rhs_count = right_sides.shape[0]
    device_count = tree_order.shape[0]
    blocks = right_sides.reshape(rhs_count, device_count, -1)
    ordered = jnp.take_along_axis(blocks, jnp.broadcast_to(tree_order[None], blocks.shape), axis=2)
    leaf_size = leaf_inverse.shape[1]
    pieces = ordered.reshape(rhs_count, -1, leaf_size)
    field = jnp.einsum('rbl,bkl->rbk', pieces, leaf_inverse, precision=HIGH).reshape(rhs_count, -1)
    field = apply_level(field, reduce_low, expand_low, coupling_low, 3)
    field = apply_level(field, reduce_mid, expand_mid, coupling_mid, 2)
    field = apply_level(field, reduce_top, expand_top, coupling_top, 1)
    field = field.reshape(rhs_count, device_count, -1)
    device_rows = jnp.arange(device_count, dtype=jnp.int32)[:, None]
    result = jnp.zeros_like(field).at[:, device_rows, tree_order].set(field)
    return result.reshape(rhs_count, -1)
```

```python
import functools

import jax
import jax.numpy as jnp
from jax import lax
from jax.experimental import pallas as pl
from jax.experimental.pallas import tpu as pltpu
from jax.sharding import PartitionSpec as P

F32 = jnp.float32
BF16 = jnp.bfloat16
LANES = 128
NODES = 4


def halves(x):
    high = x.astype(BF16)
    return high, (x - high.astype(F32)).astype(BF16)


def mxu(x, y, transposed):
    dims = (((1,), (1 if transposed else 0,)), ((), ()))
    return lax.dot_general(x, y, dims, preferred_element_type=F32)


def dot3(x, y, transposed):
    rows = x[0].shape[0]
    both = mxu(jnp.concatenate([x[0], x[1]], axis=0), y[0], transposed)
    return both[:rows] + both[rows:] + mxu(x[0], y[1], transposed)


def pick(source, index):
    rows, columns = source.shape[0], source.shape[1]
    block = index // LANES
    place = jnp.broadcast_to(index - block * LANES, (rows, LANES))
    picked = jnp.zeros((rows, LANES), F32)
    for c in range(columns // LANES):
        part = jnp.take_along_axis(source[:, c * LANES : (c + 1) * LANES], place, axis=1)
        picked = jnp.where(block == c, part, picked)
    return picked


def kernel(
    clusters,
    inners,
    rhs_hbm,
    order_hbm,
    leaf_hbm,
    rlow_hbm,
    elow_hbm,
    rmid_hbm,
    emid_hbm,
    rtop_hbm,
    etop_hbm,
    klow_hbm,
    kmid_hbm,
    ktop_hbm,
    out_ref,
    rhs,
    order,
    leaf,
    rlow,
    elow,
    rmid,
    emid,
    rtop,
    etop,
    klow,
    kmid,
    ktop,
    field,
    field_high,
    field_low,
    ordered,
    buf_a,
    buf_g,
    src_b,
    buf_b,
    buf_c,
    buf_e,
    buf_f,
    load_sem,
    leaf_sem,
    send_sem,
    recv_sem,
    node_send,
    node_recv,
):
    rhs_count, columns = rhs.shape
    leafs, size = leaf.shape[0], leaf.shape[1]
    rank = rlow.shape[0]
    cluster, inner = lax.axis_index("cluster"), lax.axis_index("inner")
    per_node = clusters // NODES
    members = per_node * inners
    rows = rhs_count // members
    node = cluster // per_node
    place = lax.rem(cluster, per_node) * inners + inner

    def device(n, q):
        return {"cluster": n * per_node + q // inners, "inner": lax.rem(q, inners)}

    barrier = pltpu.get_barrier_semaphore()
    for step in range(1, members):
        pl.semaphore_signal(
            barrier,
            inc=1,
            device_id=device(node, lax.rem(place + step, members)),
            device_id_type=pl.DeviceIdType.MESH,
        )
    for step in range(1, NODES):
        pl.semaphore_signal(
            barrier,
            inc=1,
            device_id=device(lax.rem(node + step, NODES), place),
            device_id_type=pl.DeviceIdType.MESH,
        )

    low_half = place // (members // 2)
    mid_half = lax.rem(node, 2)
    top_half = node // 2

    def load(src, dst, sem):
        copy = pltpu.make_async_copy(src, dst, sem)
        copy.start()
        return copy

    order_copy = load(order_hbm, order, load_sem.at[0])
    rhs_copy = load(rhs_hbm, rhs, load_sem.at[1])
    leaf_copies = [load(leaf_hbm.at[b], leaf.at[b], leaf_sem.at[b]) for b in range(leafs)]
    rlow_copy = load(rlow_hbm, rlow, load_sem.at[2])
    rmid_copy = load(rmid_hbm, rmid, load_sem.at[3])
    rtop_copy = load(rtop_hbm, rtop, load_sem.at[4])
    klow_copy = load(
        klow_hbm.at[node, pl.ds(pl.multiple_of(low_half * rank, rank), rank)], klow, load_sem.at[5]
    )
    elow_copy = load(elow_hbm, elow, load_sem.at[6])
    emid_copy = load(emid_hbm, emid, load_sem.at[7])
    kmid_copy = load(kmid_hbm.at[node // 2], kmid, load_sem.at[8])
    ktop_copy = load(
        ktop_hbm.at[0, pl.ds(pl.multiple_of(top_half * rank, rank), rank)], ktop, load_sem.at[9]
    )
    etop_copy = load(etop_hbm, etop, load_sem.at[10])

    def swap(kind, src_of, dst_of):
        copies = []
        for step in range(1, members):
            to = lax.rem(place + step, members)
            copies.append(
                pltpu.make_async_remote_copy(
                    src_ref=src_of(to),
                    dst_ref=dst_of(place),
                    send_sem=send_sem.at[kind, step],
                    recv_sem=recv_sem.at[kind, step],
                    device_id=device(node, to),
                    device_id_type=pl.DeviceIdType.MESH,
                )
            )
            copies[-1].start()
        return copies

    def node_swap(kind, src, dst, to):
        copy = pltpu.make_async_remote_copy(
            src_ref=src,
            dst_ref=dst,
            send_sem=node_send.at[kind],
            recv_sem=node_recv.at[kind],
            device_id=device(to, place),
            device_id_type=pl.DeviceIdType.MESH,
        )
        copy.start()
        return copy

    order_copy.wait()
    rhs_copy.wait()
    for b in range(columns // LANES):
        cols = slice(b * LANES, (b + 1) * LANES)
        ordered[:, cols] = pick(rhs[...], order[:, cols])
    for b in range(leafs):
        cols = slice(b * size, (b + 1) * size)
        leaf_copies[b].wait()
        piece = dot3(halves(ordered[:, cols]), halves(leaf[b]), True)
        field[:, cols] = piece
        field_high[:, cols], field_low[:, cols] = halves(piece)

    def coefficients(basis):
        total = jnp.zeros((rhs_count, rank), F32)
        for b in range(leafs):
            cols = slice(b * size, (b + 1) * size)
            total += dot3(
                (field_high[:, cols], field_low[:, cols]), halves(basis[:, cols]), True
            )
        return total

    rlow_copy.wait()
    coeff_low = coefficients(rlow)
    buf_a[place] = coeff_low
    pl.semaphore_wait(barrier, members - 1 + NODES - 1)
    copies_a = swap(0, lambda to: buf_a.at[place], lambda q: buf_a.at[q])

    rtop_copy.wait()
    emid_copy.wait()

    def gram(expand, reduce):
        total = jnp.zeros((rank, rank), F32)
        for b in range(leafs):
            cols = slice(b * size, (b + 1) * size)
            total += dot3(halves(expand[:, cols]), halves(reduce[:, cols]), True)
        return total

    buf_g[place] = gram(emid, rtop)
    copies_g = swap(1, lambda to: buf_g.at[place], lambda q: buf_g.at[q])
    rmid_copy.wait()
    elow_copy.wait()
    gram_mid = gram(elow, rmid)
    gram_top = gram(elow, rtop)
    coeff_mid = coefficients(rmid)
    coeff_top = coefficients(rtop)

    def total_of(buf, first, count):
        total = buf[first]
        for q in range(first + 1, first + count):
            total += buf[q]
        return total

    for copy in copies_a:
        copy.wait()
    klow_copy.wait()
    half = members // 2
    stacked = jnp.concatenate([total_of(buf_a, 0, half), total_of(buf_a, half, half)], axis=1)
    solved_low = halves(dot3(halves(stacked), halves(klow[...]), True))
    corrected = jnp.concatenate(
        [
            coeff_mid - dot3(solved_low, halves(gram_mid), False),
            coeff_top - dot3(solved_low, halves(gram_top), False),
        ],
        axis=1,
    )
    for q in range(members):
        src_b[q] = corrected[q * rows : (q + 1) * rows]
    copies_b = swap(2, lambda to: src_b.at[to], lambda q: buf_b.at[q])
    buf_b[place] = src_b[place]

    own = order[...]
    count = columns // LANES
    position = lax.broadcasted_iota(jnp.int32, (1, columns), 1)
    spots = lax.broadcasted_iota(jnp.int32, (count, columns), 0)
    hit = own // LANES == spots
    upper = jnp.where(hit, position // 16, 0).astype(F32).astype(BF16)
    lower = jnp.where(hit, lax.rem(position, 16), 0).astype(F32).astype(BF16)
    lanes = lax.broadcasted_iota(jnp.int32, (LANES, columns), 0)
    lane_hit = jnp.where(lax.rem(own, LANES) == lanes, 1.0, 0.0).astype(BF16)
    table = mxu(jnp.concatenate([upper, lower], axis=0), lane_hit, True)
    inverse = (table[:count] * 16.0 + table[count:]).astype(jnp.int32)

    for copy in copies_b:
        copy.wait()
    summed = total_of(buf_b, 0, members)
    coeff_mid_node = summed[:, :rank]
    buf_c[mid_half] = coeff_mid_node
    pair = node + 1 - 2 * mid_half
    copy_c = node_swap(0, buf_c.at[mid_half], buf_c.at[mid_half], pair)

    for b in range(leafs):
        cols = slice(b * size, (b + 1) * size)
        field[:, cols] -= dot3(solved_low, halves(elow[:, cols]), False)

    for copy in copies_g:
        copy.wait()
    kmid_copy.wait()
    gram_node = halves(total_of(buf_g, 0, members))
    kmid_half = halves(kmid[pl.ds(pl.multiple_of(mid_half * rank, rank), rank), :])
    copy_c.wait()
    stacked = jnp.concatenate([buf_c[0], buf_c[1]], axis=1)
    solved_mid = dot3(halves(stacked), kmid_half, True)
    coeff_top_node = summed[:, rank:] - dot3(halves(solved_mid), gram_node, False)
    buf_e[node] = coeff_top_node
    copies_e = [
        node_swap(step, buf_e.at[node], buf_e.at[node], lax.rem(node + step, NODES))
        for step in range(1, NODES)
    ]
    ktop_copy.wait()
    ktop_half = halves(ktop[...])
    for copy in copies_e:
        copy.wait()
    stacked = jnp.concatenate([buf_e[0] + buf_e[1], buf_e[2] + buf_e[3]], axis=1)
    solved_top = dot3(halves(stacked), ktop_half, True)
    buf_f[place] = jnp.concatenate([solved_mid, solved_top], axis=1)
    copies_f = swap(3, lambda to: buf_f.at[place], lambda q: buf_f.at[q])
    etop_copy.wait()
    for copy in copies_f:
        copy.wait()
    solved = jnp.concatenate([buf_f[q] for q in range(members)], axis=0)
    solved = halves(solved)
    for b in range(leafs):
        cols = slice(b * size, (b + 1) * size)
        expand = jnp.concatenate([emid[:, cols], etop[:, cols]], axis=0)
        field[:, cols] -= dot3(solved, halves(expand), False)
    for b in range(count):
        out_ref[:, b * LANES : (b + 1) * LANES] = pick(field[...], inverse[b : b + 1])


def on_device(
    right_sides,
    tree_order,
    leaf_inverse,
    reduce_low,
    expand_low,
    reduce_mid,
    expand_mid,
    reduce_top,
    expand_top,
    coupling_low,
    coupling_mid,
    coupling_top,
):
    rhs_count, columns = right_sides.shape
    rank = reduce_low.shape[0]
    clusters, inners = lax.axis_size("cluster"), lax.axis_size("inner")
    members = clusters // NODES * inners
    rows = rhs_count // members
    basis = pltpu.VMEM((rank, columns), F32)
    steps = max(members, NODES)
    scratch = [
        pltpu.VMEM((rhs_count, columns), F32),
        pltpu.VMEM((1, columns), jnp.int32),
        pltpu.VMEM(leaf_inverse.shape, F32),
        basis,
        basis,
        basis,
        basis,
        basis,
        basis,
        pltpu.VMEM((rank, 2 * rank), F32),
        pltpu.VMEM((2 * rank, 2 * rank), F32),
        pltpu.VMEM((rank, 2 * rank), F32),
        pltpu.VMEM((rhs_count, columns), F32),
        pltpu.VMEM((rhs_count, columns), BF16),
        pltpu.VMEM((rhs_count, columns), BF16),
        pltpu.VMEM((rhs_count, columns), F32),
        pltpu.VMEM((members, rhs_count, rank), F32),
        pltpu.VMEM((members, rank, rank), F32),
        pltpu.VMEM((members, rows, 2 * rank), F32),
        pltpu.VMEM((members, rows, 2 * rank), F32),
        pltpu.VMEM((2, rows, rank), F32),
        pltpu.VMEM((NODES, rows, rank), F32),
        pltpu.VMEM((members, rows, 2 * rank), F32),
        pltpu.SemaphoreType.DMA((11,)),
        pltpu.SemaphoreType.DMA((leaf_inverse.shape[0],)),
        pltpu.SemaphoreType.DMA((4, steps)),
        pltpu.SemaphoreType.DMA((4, steps)),
        pltpu.SemaphoreType.DMA((NODES,)),
        pltpu.SemaphoreType.DMA((NODES,)),
    ]
    return pl.pallas_call(
        functools.partial(kernel, clusters, inners),
        out_shape=jax.ShapeDtypeStruct((rhs_count, columns), F32),
        in_specs=[pl.BlockSpec(memory_space=pl.ANY)] * 12,
        out_specs=pl.BlockSpec(memory_space=pltpu.VMEM),
        scratch_shapes=scratch,
        compiler_params=pltpu.CompilerParams(
            collective_id=0, has_side_effects=True, vmem_limit_bytes=50 * 1024 * 1024
        ),
    )(
        right_sides,
        tree_order,
        leaf_inverse,
        reduce_low,
        expand_low,
        reduce_mid,
        expand_mid,
        reduce_top,
        expand_top,
        coupling_low,
        coupling_mid,
        coupling_top,
    )


def solution(mesh):
    in_specs = (
        P(None, ("groups", "cluster", "inner")),
        P(("cluster", "inner"), None),
        P(("cluster", "inner"), None, None),
        P(None, ("cluster", "inner")),
        P(None, ("cluster", "inner")),
        P(None, ("cluster", "inner")),
        P(None, ("cluster", "inner")),
        P(None, ("cluster", "inner")),
        P(None, ("cluster", "inner")),
        P(),
        P(),
        P(),
    )
    out_specs = P(None, ("groups", "cluster", "inner"))
    return jax.shard_map(
        on_device, mesh=mesh, in_specs=in_specs, out_specs=out_specs, check_vma=False
    )
```

```python
import functools

import jax
import jax.numpy as jnp
from jax import lax
from jax.experimental import pallas as pl
from jax.experimental.pallas import tpu as pltpu
from jax.sharding import PartitionSpec as P

F32 = jnp.float32
BF16 = jnp.bfloat16
LANES = 128
NODES = 4


def halves(x):
    high = x.astype(BF16)
    return high, (x - high.astype(F32)).astype(BF16)


def mxu(x, y, transposed):
    dims = (((1,), (1 if transposed else 0,)), ((), ()))
    return lax.dot_general(x, y, dims, preferred_element_type=F32)


def dot3(x, y, transposed):
    rows = x[0].shape[0]
    both = mxu(jnp.concatenate([x[0], x[1]], axis=0), y[0], transposed)
    return both[:rows] + both[rows:] + mxu(x[0], y[1], transposed)


def pick(source, index):
    rows, columns = source.shape[0], source.shape[1]
    block = index // LANES
    place = jnp.broadcast_to(index - block * LANES, (rows, LANES))
    picked = jnp.zeros((rows, LANES), F32)
    for c in range(columns // LANES):
        part = jnp.take_along_axis(source[:, c * LANES : (c + 1) * LANES], place, axis=1)
        picked = jnp.where(block == c, part, picked)
    return picked


def kernel(
    clusters,
    inners,
    rhs_hbm,
    order_hbm,
    leaf_hbm,
    rlow_hbm,
    elow_hbm,
    rmid_hbm,
    emid_hbm,
    rtop_hbm,
    etop_hbm,
    klow_hbm,
    kmid_hbm,
    ktop_hbm,
    out_ref,
    rhs,
    order,
    leaf,
    rlow,
    elow,
    rmid,
    emid,
    rtop,
    etop,
    klow,
    kmid,
    ktop,
    field,
    field_high,
    field_low,
    ordered,
    mine,
    buf_rows,
    src_low,
    buf_low,
    src_child,
    buf_child,
    buf_pair,
    src_top,
    buf_top,
    buf_nodes,
    buf_all,
    buf_mid,
    all_mid,
    buf_last,
    load_sem,
    leaf_sem,
    send_sem,
    recv_sem,
    node_send,
    node_recv,
):
    rhs_count, columns = rhs.shape
    leafs, size = leaf.shape[0], leaf.shape[1]
    rank = rlow.shape[0]
    cluster, inner = lax.axis_index("cluster"), lax.axis_index("inner")
    per_node = clusters // NODES
    members = per_node * inners
    rows = rhs_count // members
    node = cluster // per_node
    place = lax.rem(cluster, per_node) * inners + inner

    def device(n, q):
        return {"cluster": n * per_node + q // inners, "inner": lax.rem(q, inners)}

    barrier = pltpu.get_barrier_semaphore()
    for step in range(1, members):
        pl.semaphore_signal(
            barrier,
            inc=1,
            device_id=device(node, lax.rem(place + step, members)),
            device_id_type=pl.DeviceIdType.MESH,
        )
    for step in range(1, NODES):
        pl.semaphore_signal(
            barrier,
            inc=1,
            device_id=device(lax.rem(node + step, NODES), place),
            device_id_type=pl.DeviceIdType.MESH,
        )

    low_half = place // (members // 2)
    top_half = node // 2

    def load(src, dst, sem):
        copy = pltpu.make_async_copy(src, dst, sem)
        copy.start()
        return copy

    elow_copy = load(elow_hbm, elow, load_sem.at[0])
    rmid_copy = load(rmid_hbm, rmid, load_sem.at[1])
    rtop_copy = load(rtop_hbm, rtop, load_sem.at[2])
    order_copy = load(order_hbm, order, load_sem.at[3])
    rhs_copy = load(rhs_hbm, rhs, load_sem.at[4])
    emid_copy = load(emid_hbm, emid, load_sem.at[5])
    leaf_copies = [load(leaf_hbm.at[b], leaf.at[b], leaf_sem.at[b]) for b in range(leafs)]
    rlow_copy = load(rlow_hbm, rlow, load_sem.at[6])
    klow_copy = load(klow_hbm.at[node], klow, load_sem.at[7])
    kmid_copy = load(kmid_hbm, kmid, load_sem.at[8])
    ktop_copy = load(
        ktop_hbm.at[0, pl.ds(pl.multiple_of(top_half * rank, rank), rank)], ktop, load_sem.at[9]
    )
    etop_copy = load(etop_hbm, etop, load_sem.at[10])

    def swap(kind, src_of, dst, first, size):
        copies = []
        for step in range(1, size):
            to = first + lax.rem(place - first + step, size)
            copies.append(
                pltpu.make_async_remote_copy(
                    src_ref=src_of(to),
                    dst_ref=dst,
                    send_sem=send_sem.at[kind, step],
                    recv_sem=recv_sem.at[kind, step],
                    device_id=device(node, to),
                    device_id_type=pl.DeviceIdType.MESH,
                )
            )
            copies[-1].start()
        return copies

    def node_swap(kind, ref):
        copies = []
        for step in range(1, NODES):
            copies.append(
                pltpu.make_async_remote_copy(
                    src_ref=ref,
                    dst_ref=ref,
                    send_sem=node_send.at[kind, step],
                    recv_sem=node_recv.at[kind, step],
                    device_id=device(lax.rem(node + step, NODES), place),
                    device_id_type=pl.DeviceIdType.MESH,
                )
            )
            copies[-1].start()
        return copies

    def finish(copies):
        for copy in copies:
            copy.wait()

    def total_of(buf, first, count):
        total = buf[first]
        for q in range(first + 1, first + count):
            total += buf[q]
        return total

    def gram(expand, reduce):
        total = jnp.zeros((rank, rank), F32)
        for b in range(leafs):
            cols = slice(b * size, (b + 1) * size)
            total += dot3(halves(expand[:, cols]), halves(reduce[:, cols]), True)
        return total

    half = members // 2
    base = low_half * half
    part = rank // half
    slab = rank // members

    elow_copy.wait()
    rmid_copy.wait()
    rtop_copy.wait()
    grams = jnp.concatenate([gram(elow, rmid), gram(elow, rtop)], axis=1)
    for j in range(half):
        src_child[j] = grams[j * part : (j + 1) * part]
    pl.semaphore_wait(barrier, members - 1 + NODES - 1)
    copies_child = swap(
        0, lambda to: src_child.at[to - base], buf_child.at[place - base], base, half
    )
    buf_child[place - base] = src_child[place - base]
    emid_copy.wait()
    gram_node = gram(emid, rtop)
    for q in range(members):
        src_top[q] = gram_node[q * slab : (q + 1) * slab]
    copies_top = swap(1, lambda to: src_top.at[to], buf_top.at[place], 0, members)
    buf_top[place] = src_top[place]

    order_copy.wait()
    rhs_copy.wait()
    blocks = columns // LANES
    for b in range(blocks):
        cols = slice(b * LANES, (b + 1) * LANES)
        ordered[:, cols] = pick(rhs[...], order[:, cols])
        if b == blocks // 2:
            finish(copies_child)
            buf_pair[place] = total_of(buf_child, 0, half)
            copies_pair = swap(2, lambda to: buf_pair.at[place], buf_pair.at[place], 0, members)
    finish(copies_top)
    buf_nodes[node] = total_of(buf_top, 0, members)
    copies_nodes = node_swap(0, buf_nodes.at[node])
    for b in range(leafs):
        cols = slice(b * size, (b + 1) * size)
        leaf_copies[b].wait()
        piece = dot3(halves(ordered[:, cols]), halves(leaf[b]), True)
        field[:, cols] = piece
        field_high[:, cols], field_low[:, cols] = halves(piece)

    def coefficients(basis):
        total = jnp.zeros((rhs_count, rank), F32)
        for b in range(leafs):
            cols = slice(b * size, (b + 1) * size)
            total += dot3(
                (field_high[:, cols], field_low[:, cols]), halves(basis[:, cols]), True
            )
        return total

    rlow_copy.wait()
    for k, basis in enumerate((rlow, rmid, rtop)):
        coeff = coefficients(basis)
        for q in range(members):
            mine[q, :, k * rank : (k + 1) * rank] = coeff[q * rows : (q + 1) * rows]
    copies_rows = swap(3, lambda to: mine.at[to], buf_rows.at[place], 0, members)
    buf_rows[place] = mine[place]
    finish(copies_nodes)
    copies_all = swap(4, lambda to: buf_nodes, buf_all.at[place], 0, members)
    buf_all[place] = buf_nodes[...]

    klow_copy.wait()
    klow_parts = halves(klow[...])
    finish(copies_pair)
    pair_parts = halves(jnp.concatenate([buf_pair[q] for q in range(members)], axis=0))
    finish(copies_rows)
    first, second = total_of(buf_rows, 0, half), total_of(buf_rows, half, half)
    stacked = jnp.concatenate([first[:, :rank], second[:, :rank]], axis=1)
    solved = dot3(halves(stacked), klow_parts, True)
    later = first[:, rank:] + second[:, rank:]
    buf_mid[node] = later - dot3(halves(solved), pair_parts, False)
    copies_mid = node_swap(1, buf_mid.at[node])
    src_low[0] = solved[:, :rank]
    src_low[1] = solved[:, rank:]
    copies_low = swap(5, lambda to: src_low.at[to // half], buf_low.at[place], 0, members)
    buf_low[place] = src_low[low_half]

    own = order[...]
    count = columns // LANES
    position = lax.broadcasted_iota(jnp.int32, (1, columns), 1)
    spots = lax.broadcasted_iota(jnp.int32, (count, columns), 0)
    hit = own // LANES == spots
    upper = jnp.where(hit, position // 16, 0).astype(F32).astype(BF16)
    lower = jnp.where(hit, lax.rem(position, 16), 0).astype(F32).astype(BF16)
    lanes = lax.broadcasted_iota(jnp.int32, (LANES, columns), 0)
    lane_hit = jnp.where(lax.rem(own, LANES) == lanes, 1.0, 0.0).astype(BF16)
    table = mxu(jnp.concatenate([upper, lower], axis=0), lane_hit, True)
    inverse = (table[:count] * 16.0 + table[count:]).astype(jnp.int32)

    kmid_copy.wait()
    ktop_copy.wait()
    kmid_parts = [halves(kmid[n]) for n in range(NODES // 2)]
    ktop_parts = halves(ktop[...])
    finish(copies_low)
    solved_low = halves(jnp.concatenate([buf_low[q] for q in range(members)], axis=0))
    for b in range(leafs):
        cols = slice(b * size, (b + 1) * size)
        field[:, cols] -= dot3(solved_low, halves(elow[:, cols]), False)
    finish(copies_all)
    all_parts = [
        halves(
            jnp.concatenate(
                [buf_all[q, 2 * n + k] for k in range(2) for q in range(members)], axis=0
            )
        )
        for n in range(NODES // 2)
    ]
    finish(copies_mid)
    tops = []
    for n in range(NODES // 2):
        left, right = buf_mid[2 * n], buf_mid[2 * n + 1]
        stacked = jnp.concatenate([left[:, :rank], right[:, :rank]], axis=1)
        solved = dot3(halves(stacked), kmid_parts[n], True)
        all_mid[2 * n] = solved[:, :rank]
        all_mid[2 * n + 1] = solved[:, rank:]
        later = left[:, rank:] + right[:, rank:]
        tops.append(later - dot3(halves(solved), all_parts[n], False))
    solved_top = dot3(halves(jnp.concatenate(tops, axis=1)), ktop_parts, True)
    buf_last[place] = jnp.concatenate([all_mid[node], solved_top], axis=1)
    copies_last = swap(6, lambda to: buf_last.at[place], buf_last.at[place], 0, members)
    etop_copy.wait()
    finish(copies_last)
    solved = jnp.concatenate([buf_last[q] for q in range(members)], axis=0)
    solved = halves(solved)
    for b in range(leafs):
        cols = slice(b * size, (b + 1) * size)
        expand = jnp.concatenate([emid[:, cols], etop[:, cols]], axis=0)
        field[:, cols] -= dot3(solved, halves(expand), False)
    for b in range(count):
        out_ref[:, b * LANES : (b + 1) * LANES] = pick(field[...], inverse[b : b + 1])


def on_device(
    right_sides,
    tree_order,
    leaf_inverse,
    reduce_low,
    expand_low,
    reduce_mid,
    expand_mid,
    reduce_top,
    expand_top,
    coupling_low,
    coupling_mid,
    coupling_top,
):
    rhs_count, columns = right_sides.shape
    rank = reduce_low.shape[0]
    clusters, inners = lax.axis_size("cluster"), lax.axis_size("inner")
    members = clusters // NODES * inners
    rows = rhs_count // members
    basis = pltpu.VMEM((rank, columns), F32)
    half = members // 2
    slab = rank // members
    scratch = [
        pltpu.VMEM((rhs_count, columns), F32),
        pltpu.VMEM((1, columns), jnp.int32),
        pltpu.VMEM(leaf_inverse.shape, F32),
        basis,
        basis,
        basis,
        basis,
        basis,
        basis,
        pltpu.VMEM((2 * rank, 2 * rank), F32),
        pltpu.VMEM((NODES // 2, 2 * rank, 2 * rank), F32),
        pltpu.VMEM((rank, 2 * rank), F32),
        pltpu.VMEM((rhs_count, columns), F32),
        pltpu.VMEM((rhs_count, columns), BF16),
        pltpu.VMEM((rhs_count, columns), BF16),
        pltpu.VMEM((rhs_count, columns), F32),
        pltpu.VMEM((members, rows, 3 * rank), F32),
        pltpu.VMEM((members, rows, 3 * rank), F32),
        pltpu.VMEM((2, rows, rank), F32),
        pltpu.VMEM((members, rows, rank), F32),
        pltpu.VMEM((half, rank // half, 2 * rank), F32),
        pltpu.VMEM((half, rank // half, 2 * rank), F32),
        pltpu.VMEM((members, rank // half, 2 * rank), F32),
        pltpu.VMEM((members, slab, rank), F32),
        pltpu.VMEM((members, slab, rank), F32),
        pltpu.VMEM((NODES, slab, rank), F32),
        pltpu.VMEM((members, NODES, slab, rank), F32),
        pltpu.VMEM((NODES, rows, 2 * rank), F32),
        pltpu.VMEM((NODES, rows, rank), F32),
        pltpu.VMEM((members, rows, 2 * rank), F32),
        pltpu.SemaphoreType.DMA((11,)),
        pltpu.SemaphoreType.DMA((leaf_inverse.shape[0],)),
        pltpu.SemaphoreType.DMA((7, members)),
        pltpu.SemaphoreType.DMA((7, members)),
        pltpu.SemaphoreType.DMA((2, NODES)),
        pltpu.SemaphoreType.DMA((2, NODES)),
    ]
    return pl.pallas_call(
        functools.partial(kernel, clusters, inners),
        out_shape=jax.ShapeDtypeStruct((rhs_count, columns), F32),
        in_specs=[pl.BlockSpec(memory_space=pl.ANY)] * 12,
        out_specs=pl.BlockSpec(memory_space=pltpu.VMEM),
        scratch_shapes=scratch,
        compiler_params=pltpu.CompilerParams(
            collective_id=0, has_side_effects=True, vmem_limit_bytes=63 * 1024 * 1024
        ),
    )(
        right_sides,
        tree_order,
        leaf_inverse,
        reduce_low,
        expand_low,
        reduce_mid,
        expand_mid,
        reduce_top,
        expand_top,
        coupling_low,
        coupling_mid,
        coupling_top,
    )


def solution(mesh):
    in_specs = (
        P(None, ("groups", "cluster", "inner")),
        P(("cluster", "inner"), None),
        P(("cluster", "inner"), None, None),
        P(None, ("cluster", "inner")),
        P(None, ("cluster", "inner")),
        P(None, ("cluster", "inner")),
        P(None, ("cluster", "inner")),
        P(None, ("cluster", "inner")),
        P(None, ("cluster", "inner")),
        P(),
        P(),
        P(),
    )
    out_specs = P(None, ("groups", "cluster", "inner"))
    return jax.shard_map(
        on_device, mesh=mesh, in_specs=in_specs, out_specs=out_specs, check_vma=False
    )
```

```python
import functools

import jax
import jax.numpy as jnp
from jax import lax
from jax.experimental import pallas as pl
from jax.experimental.pallas import tpu as pltpu
from jax.sharding import PartitionSpec as P

F32 = jnp.float32
BF16 = jnp.bfloat16
LANES = 128
NODES = 4


def halves(x):
    high = x.astype(BF16)
    return high, (x - high.astype(F32)).astype(BF16)


def mxu(x, y, transposed):
    dims = (((1,), (1 if transposed else 0,)), ((), ()))
    return lax.dot_general(x, y, dims, preferred_element_type=F32)


def dot3(x, y, transposed):
    rows = x[0].shape[0]
    both = mxu(jnp.concatenate([x[0], x[1]], axis=0), y[0], transposed)
    return both[:rows] + both[rows:] + mxu(x[0], y[1], transposed)


def pick(source, index):
    rows, columns = source.shape[0], source.shape[1]
    block = index // LANES
    place = jnp.broadcast_to(index - block * LANES, (rows, LANES))
    picked = jnp.zeros((rows, LANES), F32)
    for c in range(columns // LANES):
        part = jnp.take_along_axis(source[:, c * LANES : (c + 1) * LANES], place, axis=1)
        picked = jnp.where(block == c, part, picked)
    return picked


def kernel(
    clusters,
    inners,
    rhs_hbm,
    order_hbm,
    leaf_hbm,
    rlow_hbm,
    elow_hbm,
    rmid_hbm,
    emid_hbm,
    rtop_hbm,
    etop_hbm,
    klow_hbm,
    kmid_hbm,
    ktop_hbm,
    out_ref,
    rhs,
    order,
    leaf,
    rlow,
    elow,
    rmid,
    emid,
    rtop,
    etop,
    klow,
    kmid,
    ktop,
    field,
    field_high,
    field_low,
    ordered,
    mine,
    buf_rows,
    src_low,
    buf_low,
    src_child,
    buf_child,
    buf_pair,
    src_top,
    buf_top,
    buf_nodes,
    buf_all,
    buf_mid,
    all_mid,
    buf_last,
    load_sem,
    leaf_sem,
    send_sem,
    recv_sem,
    node_send,
    node_recv,
):
    rhs_count, columns = rhs.shape
    leafs, size = leaf.shape[0], leaf.shape[1]
    rank = rlow.shape[0]
    cluster, inner = lax.axis_index("cluster"), lax.axis_index("inner")
    per_node = clusters // NODES
    members = per_node * inners
    rows = rhs_count // members
    node = cluster // per_node
    place = lax.rem(cluster, per_node) * inners + inner

    def device(n, q):
        return {"cluster": n * per_node + q // inners, "inner": lax.rem(q, inners)}

    barrier = pltpu.get_barrier_semaphore()
    for step in range(1, members):
        pl.semaphore_signal(
            barrier,
            inc=1,
            device_id=device(node, lax.rem(place + step, members)),
            device_id_type=pl.DeviceIdType.MESH,
        )
    for step in range(1, NODES):
        pl.semaphore_signal(
            barrier,
            inc=1,
            device_id=device(lax.rem(node + step, NODES), place),
            device_id_type=pl.DeviceIdType.MESH,
        )

    low_half = place // (members // 2)
    top_half = node // 2

    def load(src, dst, sem):
        copy = pltpu.make_async_copy(src, dst, sem)
        copy.start()
        return copy

    elow_copy = load(elow_hbm, elow, load_sem.at[0])
    rmid_copy = load(rmid_hbm, rmid, load_sem.at[1])
    rtop_copy = load(rtop_hbm, rtop, load_sem.at[2])
    order_copy = load(order_hbm, order, load_sem.at[3])
    rhs_copy = load(rhs_hbm, rhs, load_sem.at[4])
    emid_copy = load(emid_hbm, emid, load_sem.at[5])
    leaf_copies = [load(leaf_hbm.at[b], leaf.at[b], leaf_sem.at[b]) for b in range(leafs)]
    rlow_copy = load(rlow_hbm, rlow, load_sem.at[6])
    klow_copy = load(klow_hbm.at[node], klow, load_sem.at[7])
    kmid_copy = load(kmid_hbm, kmid, load_sem.at[8])
    ktop_copy = load(
        ktop_hbm.at[0, pl.ds(pl.multiple_of(top_half * rank, rank), rank)], ktop, load_sem.at[9]
    )
    etop_copy = load(etop_hbm, etop, load_sem.at[10])

    def swap(kind, src_of, dst, first, size):
        copies = []
        for step in range(1, size):
            to = first + lax.rem(place - first + step, size)
            copies.append(
                pltpu.make_async_remote_copy(
                    src_ref=src_of(to),
                    dst_ref=dst,
                    send_sem=send_sem.at[kind, step],
                    recv_sem=recv_sem.at[kind, step],
                    device_id=device(node, to),
                    device_id_type=pl.DeviceIdType.MESH,
                )
            )
            copies[-1].start()
        return copies

    def node_swap(kind, ref):
        copies = []
        for step in range(1, NODES):
            copies.append(
                pltpu.make_async_remote_copy(
                    src_ref=ref,
                    dst_ref=ref,
                    send_sem=node_send.at[kind, step],
                    recv_sem=node_recv.at[kind, step],
                    device_id=device(lax.rem(node + step, NODES), place),
                    device_id_type=pl.DeviceIdType.MESH,
                )
            )
            copies[-1].start()
        return copies

    def finish(copies):
        for copy in copies:
            copy.wait()

    def total_of(buf, first, count):
        total = buf[first]
        for q in range(first + 1, first + count):
            total += buf[q]
        return total

    def gram(expand, reduce):
        total = jnp.zeros((rank, rank), F32)
        for b in range(leafs):
            cols = slice(b * size, (b + 1) * size)
            total += dot3(halves(expand[:, cols]), halves(reduce[:, cols]), True)
        return total

    half = members // 2
    base = low_half * half
    part = rank // half
    slab = rank // members

    elow_copy.wait()
    rmid_copy.wait()
    rtop_copy.wait()
    grams = jnp.concatenate([gram(elow, rmid), gram(elow, rtop)], axis=1)
    for j in range(half):
        src_child[j] = grams[j * part : (j + 1) * part]
    buf_child[place - base] = src_child[place - base]
    emid_copy.wait()
    gram_node = gram(emid, rtop)
    for q in range(members):
        src_top[q] = gram_node[q * slab : (q + 1) * slab]
    buf_top[place] = src_top[place]

    order_copy.wait()
    rhs_copy.wait()
    blocks = columns // LANES
    for b in range(blocks):
        cols = slice(b * LANES, (b + 1) * LANES)
        ordered[:, cols] = pick(rhs[...], order[:, cols])
    pl.semaphore_wait(barrier, members - 1 + NODES - 1)
    copies_child = swap(
        0, lambda to: src_child.at[to - base], buf_child.at[place - base], base, half
    )
    copies_top = swap(1, lambda to: src_top.at[to], buf_top.at[place], 0, members)
    for copy in leaf_copies:
        copy.wait()
    for b in range(leafs):
        cols = slice(b * size, (b + 1) * size)
        piece = dot3(halves(ordered[:, cols]), halves(leaf[b]), True)
        field[:, cols] = piece
        field_high[:, cols], field_low[:, cols] = halves(piece)

    finish(copies_child)
    buf_pair[place] = total_of(buf_child, 0, half)
    copies_pair = swap(2, lambda to: buf_pair.at[place], buf_pair.at[place], 0, members)

    def coefficients(basis):
        total = jnp.zeros((rhs_count, rank), F32)
        for b in range(leafs):
            cols = slice(b * size, (b + 1) * size)
            total += dot3(
                (field_high[:, cols], field_low[:, cols]), halves(basis[:, cols]), True
            )
        return total

    rlow_copy.wait()
    for k, basis in enumerate((rlow, rmid, rtop)):
        if k == 2:
            finish(copies_top)
            buf_nodes[node] = total_of(buf_top, 0, members)
            copies_nodes = node_swap(0, buf_nodes.at[node])
        coeff = coefficients(basis)
        for q in range(members):
            mine[q, :, k * rank : (k + 1) * rank] = coeff[q * rows : (q + 1) * rows]
    copies_rows = swap(3, lambda to: mine.at[to], buf_rows.at[place], 0, members)
    buf_rows[place] = mine[place]
    klow_copy.wait()
    klow_parts = halves(klow[...])

    finish(copies_pair)
    pair_parts = halves(jnp.concatenate([buf_pair[q] for q in range(members)], axis=0))
    finish(copies_rows)
    first, second = total_of(buf_rows, 0, half), total_of(buf_rows, half, half)
    stacked = jnp.concatenate([first[:, :rank], second[:, :rank]], axis=1)
    solved = dot3(halves(stacked), klow_parts, True)
    later = first[:, rank:] + second[:, rank:]
    buf_mid[node] = later - dot3(halves(solved), pair_parts, False)
    copies_mid = node_swap(1, buf_mid.at[node])
    src_low[0] = solved[:, :rank]
    src_low[1] = solved[:, rank:]
    copies_low = swap(5, lambda to: src_low.at[to // half], buf_low.at[place], 0, members)
    buf_low[place] = src_low[low_half]
    finish(copies_nodes)
    copies_all = swap(4, lambda to: buf_nodes, buf_all.at[place], 0, members)
    buf_all[place] = buf_nodes[...]

    own = order[...]
    count = columns // LANES
    position = lax.broadcasted_iota(jnp.int32, (1, columns), 1)
    spots = lax.broadcasted_iota(jnp.int32, (count, columns), 0)
    hit = own // LANES == spots
    upper = jnp.where(hit, position // 16, 0).astype(F32).astype(BF16)
    lower = jnp.where(hit, lax.rem(position, 16), 0).astype(F32).astype(BF16)
    lanes = lax.broadcasted_iota(jnp.int32, (LANES, columns), 0)
    lane_hit = jnp.where(lax.rem(own, LANES) == lanes, 1.0, 0.0).astype(BF16)
    table = mxu(jnp.concatenate([upper, lower], axis=0), lane_hit, True)
    inverse = (table[:count] * 16.0 + table[count:]).astype(jnp.int32)

    kmid_copy.wait()
    ktop_copy.wait()
    kmid_parts = [halves(kmid[n]) for n in range(NODES // 2)]
    ktop_parts = halves(ktop[...])
    finish(copies_low)
    solved_low = halves(jnp.concatenate([buf_low[q] for q in range(members)], axis=0))
    for b in range(leafs):
        cols = slice(b * size, (b + 1) * size)
        field[:, cols] -= dot3(solved_low, halves(elow[:, cols]), False)
    finish(copies_all)
    all_parts = [
        halves(
            jnp.concatenate(
                [buf_all[q, 2 * n + k] for k in range(2) for q in range(members)], axis=0
            )
        )
        for n in range(NODES // 2)
    ]
    finish(copies_mid)
    tops = []
    for n in range(NODES // 2):
        left, right = buf_mid[2 * n], buf_mid[2 * n + 1]
        stacked = jnp.concatenate([left[:, :rank], right[:, :rank]], axis=1)
        solved = dot3(halves(stacked), kmid_parts[n], True)
        all_mid[2 * n] = solved[:, :rank]
        all_mid[2 * n + 1] = solved[:, rank:]
        later = left[:, rank:] + right[:, rank:]
        tops.append(later - dot3(halves(solved), all_parts[n], False))
    solved_top = dot3(halves(jnp.concatenate(tops, axis=1)), ktop_parts, True)
    buf_last[place] = jnp.concatenate([all_mid[node], solved_top], axis=1)
    copies_last = swap(6, lambda to: buf_last.at[place], buf_last.at[place], 0, members)
    etop_copy.wait()
    finish(copies_last)
    solved = jnp.concatenate([buf_last[q] for q in range(members)], axis=0)
    solved = halves(solved)
    for b in range(leafs):
        cols = slice(b * size, (b + 1) * size)
        expand = jnp.concatenate([emid[:, cols], etop[:, cols]], axis=0)
        field[:, cols] -= dot3(solved, halves(expand), False)
    for b in range(count):
        out_ref[:, b * LANES : (b + 1) * LANES] = pick(field[...], inverse[b : b + 1])


def on_device(
    right_sides,
    tree_order,
    leaf_inverse,
    reduce_low,
    expand_low,
    reduce_mid,
    expand_mid,
    reduce_top,
    expand_top,
    coupling_low,
    coupling_mid,
    coupling_top,
):
    rhs_count, columns = right_sides.shape
    rank = reduce_low.shape[0]
    clusters, inners = lax.axis_size("cluster"), lax.axis_size("inner")
    members = clusters // NODES * inners
    rows = rhs_count // members
    basis = pltpu.VMEM((rank, columns), F32)
    half = members // 2
    slab = rank // members
    scratch = [
        pltpu.VMEM((rhs_count, columns), F32),
        pltpu.VMEM((1, columns), jnp.int32),
        pltpu.VMEM(leaf_inverse.shape, F32),
        basis,
        basis,
        basis,
        basis,
        basis,
        basis,
        pltpu.VMEM((2 * rank, 2 * rank), F32),
        pltpu.VMEM((NODES // 2, 2 * rank, 2 * rank), F32),
        pltpu.VMEM((rank, 2 * rank), F32),
        pltpu.VMEM((rhs_count, columns), F32),
        pltpu.VMEM((rhs_count, columns), BF16),
        pltpu.VMEM((rhs_count, columns), BF16),
        pltpu.VMEM((rhs_count, columns), F32),
        pltpu.VMEM((members, rows, 3 * rank), F32),
        pltpu.VMEM((members, rows, 3 * rank), F32),
        pltpu.VMEM((2, rows, rank), F32),
        pltpu.VMEM((members, rows, rank), F32),
        pltpu.VMEM((half, rank // half, 2 * rank), F32),
        pltpu.VMEM((half, rank // half, 2 * rank), F32),
        pltpu.VMEM((members, rank // half, 2 * rank), F32),
        pltpu.VMEM((members, slab, rank), F32),
        pltpu.VMEM((members, slab, rank), F32),
        pltpu.VMEM((NODES, slab, rank), F32),
        pltpu.VMEM((members, NODES, slab, rank), F32),
        pltpu.VMEM((NODES, rows, 2 * rank), F32),
        pltpu.VMEM((NODES, rows, rank), F32),
        pltpu.VMEM((members, rows, 2 * rank), F32),
        pltpu.SemaphoreType.DMA((11,)),
        pltpu.SemaphoreType.DMA((leaf_inverse.shape[0],)),
        pltpu.SemaphoreType.DMA((7, members)),
        pltpu.SemaphoreType.DMA((7, members)),
        pltpu.SemaphoreType.DMA((2, NODES)),
        pltpu.SemaphoreType.DMA((2, NODES)),
    ]
    return pl.pallas_call(
        functools.partial(kernel, clusters, inners),
        out_shape=jax.ShapeDtypeStruct((rhs_count, columns), F32),
        in_specs=[pl.BlockSpec(memory_space=pl.ANY)] * 12,
        out_specs=pl.BlockSpec(memory_space=pltpu.VMEM),
        scratch_shapes=scratch,
        compiler_params=pltpu.CompilerParams(
            collective_id=0, has_side_effects=True, vmem_limit_bytes=63 * 1024 * 1024
        ),
    )(
        right_sides,
        tree_order,
        leaf_inverse,
        reduce_low,
        expand_low,
        reduce_mid,
        expand_mid,
        reduce_top,
        expand_top,
        coupling_low,
        coupling_mid,
        coupling_top,
    )


def solution(mesh):
    in_specs = (
        P(None, ("groups", "cluster", "inner")),
        P(("cluster", "inner"), None),
        P(("cluster", "inner"), None, None),
        P(None, ("cluster", "inner")),
        P(None, ("cluster", "inner")),
        P(None, ("cluster", "inner")),
        P(None, ("cluster", "inner")),
        P(None, ("cluster", "inner")),
        P(None, ("cluster", "inner")),
        P(),
        P(),
        P(),
    )
    out_specs = P(None, ("groups", "cluster", "inner"))
    return jax.shard_map(
        on_device, mesh=mesh, in_specs=in_specs, out_specs=out_specs, check_vma=False
    )
```
